256 devices in a mesh: dp: 16 (over y, x), expert: 16 (over z, core).
Axes of the slice: x: 4, y: 4, z: 8, core: 2. Of those that a mesh axis runs over, the one named last changes fastest.
Arguments:
- tokens: bfloat16 [4096, 4096], P('dp', 'expert'), may hold values from -6 to 6
- out_grads: bfloat16 [4096, 4096], P('dp', 'expert'), may hold values from -6 to 6
- routes: int32 [4096, 2], P('dp'), may hold values from 0 to 15, all different within a row; in each aligned block of 256 rows (0 to 255, 256 to 511, ...) at most 64 rows name the same one
- gate_codes: int32 [4096, 2], P('dp'), may hold values from 256 to 4095
- w_gate: bfloat16 [16, 4096, 6400], P('expert', None, 'dp'), may hold values from -0.09375 to 0.09375
- w_up: bfloat16 [16, 4096, 6400], P('expert', None, 'dp'), may hold values from -0.09375 to 0.09375
- w_down: bfloat16 [16, 6400, 4096], P('expert', 'dp'), may hold values from -0.078125 to 0.078125
- proj_in: bfloat16 [4096, 128], replicated, may hold values from -0.09375 to 0.09375
- proj_hidden: bfloat16 [6400, 192], P('dp'), may hold values from -0.078125 to 0.078125
Outputs:
- projected: float32 [16, 16, 12288], P(None, 'expert', 'dp')
The draws below stay inside these ranges and needn't reach their ends.
Inputs may be any that keep to these rules, and one draw needn't show every extreme that they name: `routes`: each row names 2 different experts. Among the rows of one sequence no expert is named more than 64 times, a bound that some block reaches.
All inputs are finite; a program needn't handle non-finite values.
Results may differ from the reference program's by a relative error of at most 0.0029.
Values may be sent and summed in bfloat16 or wider, within the bound.
No kernel may reach another device: no remote copies, remote signals or barrier semaphores. Data moves between devices by JAX's collectives and lax.ppermute only.
A program may use at most 128 MiB of HBM per device.

```python
import math
import jax
import jax.numpy as jnp
import numpy as np
from jax import lax

D = 4096
FF = 6400
TOP = 2
R = 64
LEN = 256
SEQS = 16
CAP = 64
EXPERTS = 16
TOKENS = 4096


def set_ends(array, key, low, high):
    longest = array.shape.index(max(array.shape))
    spots = []
    for shift in (0, 1):
        where = [jax.random.randint(jax.random.fold_in(key, axis), (), 0, length) for axis, length in enumerate(array.shape)]
        where[longest] = (where[longest] + shift) % array.shape[longest]
        spots.append(tuple(where))
    return array.at[spots[0]].set(low).at[spots[1]].set(high)


def level_of(key, dims, cuts, low, top_value):
    def one(axis_at, blocks):
        steps = jax.random.uniform(jax.random.fold_in(jax.random.fold_in(key, 6), axis_at), (blocks,), jnp.float32, low / len(cuts), top_value / len(cuts))
        return jnp.repeat(jnp.exp(steps), dims[axis_at] // blocks).reshape((-1,) + (1,) * (len(dims) - axis_at - 1))

    factor_of = one(*cuts[0])
    for cut in cuts[1:]:
        factor_of = factor_of * one(*cut)
    return factor_of


def deal_out(own_key, own, number, rows, number_of, top, bound, lean):
    sequence = jax.random.permutation(own_key, number_of)
    crowded, ordinary = load_shares(number_of, rows * top, bound, lean, True), load_shares(number_of, rows * top, bound, lean, False)
    places = jnp.arange(number_of)

    def named(lengths, offset_by):
        used = int((lengths > 0).sum())
        fixed = max(1, used // 4)
        moved = fixed + (places - fixed + offset_by * (used - fixed)) % max(1, number_of - fixed)
        return jnp.zeros((number_of,), jnp.int32).at[sequence[jnp.where(places < fixed, places, moved)]].set(jnp.asarray(lengths, jnp.int32))

    lengths = jnp.where(number % 4 == 0, named(crowded, number // 4), named(ordinary, number - number // 4 - 1))
    mixed = jax.random.permutation(jax.random.fold_in(own, 3), number_of)
    source_of, taker = mixed[0:number_of // 2 * 2:2], mixed[1:number_of // 2 * 2:2]
    room = jnp.minimum(lengths[source_of] - 1, bound - lengths[taker]) // 2
    room = jnp.where((source_of == sequence[0]) | (taker == sequence[0]) | (lengths[taker] == 0), 0, jnp.maximum(room, 0))
    moved = jax.random.randint(jax.random.fold_in(own, 4), (number_of // 2,), 0, 1 << 20) % (room + 1)
    lengths = lengths.at[source_of].add(-moved).at[taker].add(moved)
    items = jnp.searchsorted(jnp.cumsum(lengths), jnp.arange(rows * top), side="right").astype(jnp.int32)
    table = items.reshape(top, rows).T
    table = table[jax.random.permutation(jax.random.fold_in(own, 1), rows)]
    offset_by = jax.random.randint(jax.random.fold_in(own, 2), (rows, 1), 0, top)
    return jnp.take_along_axis(table, (jnp.arange(top)[None, :] + offset_by) % top, axis=1)


def load_shares(count, total, bound, slope, full):
    weights = [(1 << 20) // math.isqrt(grade ** slope) + 1 for grade in range(1, count + 1)]
    largest = bound if full else min(bound, max(-(-total // count), total * weights[0] // sum(weights)))
    least = 1 if total - largest >= count - 1 else 0
    counts, spare = [largest] + [least] * (count - 1), total - largest - least * (count - 1)
    while spare > 0:
        candidates = [i for i in range(1, count) if counts[i] < largest] or [i for i in range(1, count) if counts[i] < bound]
        whole, remaining = sum([weights[i] for i in candidates]), spare
        for i in candidates:
            more = min(bound - counts[i], max(1, remaining * weights[i] // whole), spare)
            counts[i] = counts[i] + more
            spare = spare - more
    return np.array(counts)


def normal_values(stream_key, extent, scale, reach, cuts=(), kind=jnp.bfloat16):
    gain = level_of(stream_key, extent, cuts, -0.22, 0.18) if cuts else 1.0
    result = jax.random.normal(stream_key, extent, jnp.float32) * scale * gain
    return jnp.minimum(jnp.maximum(result, -reach), reach).astype(kind)


def setup_inputs(seed: int = 0) -> dict:
    arg_keys = jax.random.split(jax.random.key(seed), 10)
    tokens = normal_values(arg_keys[0], (TOKENS, D), 1.0, 6.0, ((0, 16), (1, 16)))
    out_grads = normal_values(arg_keys[1], (TOKENS, D), 1.0, 6.0, ((0, 16), (1, 16)))
    routes_keys = jax.random.split(jax.random.fold_in(arg_keys[2], 1), TOKENS // LEN)
    routes_turns = jax.random.permutation(jax.random.fold_in(arg_keys[2], 3), TOKENS // LEN)
    routes = jax.vmap(lambda own, number: deal_out(jax.random.fold_in(arg_keys[2], 2), own, number, LEN, EXPERTS, TOP, CAP, 2))(routes_keys, routes_turns).reshape((TOKENS, TOP))
    gate_codes = set_ends(jax.random.randint(arg_keys[3], (TOKENS, TOP), 256, 4096), jax.random.fold_in(arg_keys[3], 1), 256, 4095).astype(jnp.int32)
    w_gate = normal_values(arg_keys[4], (EXPERTS, D, FF), D ** -0.5, 0.09375, ((0, 16), (2, 16)))
    w_up = normal_values(arg_keys[5], (EXPERTS, D, FF), D ** -0.5, 0.09375, ((0, 16), (2, 16)))
    w_down = normal_values(arg_keys[6], (EXPERTS, FF, D), FF ** -0.5, 0.078125, ((0, 16), (1, 16)))
    proj_in = normal_values(arg_keys[7], (D, 2 * R), D ** -0.5, 0.09375)
    proj_hidden = normal_values(arg_keys[8], (FF, 3 * R), FF ** -0.5, 0.078125, ((0, 16),))
    return {"tokens": tokens, "out_grads": out_grads, "routes": routes, "gate_codes": gate_codes, "w_gate": w_gate, "w_up": w_up, "w_down": w_down, "proj_in": proj_in, "proj_hidden": proj_hidden}


def expert_grads(xs, dys, weight, seq_ids, wg, wu, wd, proj_in, proj_hidden):
    rank = proj_in.shape[1] // 2
    gate = jnp.dot(xs, wg, preferred_element_type=jnp.float32)
    upper = jnp.dot(xs, wu, preferred_element_type=jnp.float32)
    sig = jax.nn.sigmoid(gate)
    act = gate * sig
    hidden = (act * upper).astype(jnp.bfloat16)
    back = lax.dot_general(dys, wd, (((1,), (1,)), ((), ())), preferred_element_type=jnp.float32) * weight[:, None]
    d_up = (back * act).astype(jnp.bfloat16)
    d_gate = (back * upper * sig * (1.0 + gate * (1.0 - sig))).astype(jnp.bfloat16)
    in_proj = jnp.dot(xs, proj_in[:, :rank], preferred_element_type=jnp.float32)
    out_proj = jnp.dot(dys, proj_in[:, rank:], preferred_element_type=jnp.float32) * weight[:, None]
    hid_proj = jnp.dot(hidden, proj_hidden[:, :rank], preferred_element_type=jnp.float32)
    gate_proj = jnp.dot(d_gate, proj_hidden[:, rank:2 * rank], preferred_element_type=jnp.float32)
    up_proj = jnp.dot(d_up, proj_hidden[:, 2 * rank:], preferred_element_type=jnp.float32)
    onehot = (seq_ids[:, None] == jnp.arange(SEQS, dtype=jnp.int32)[None, :]).astype(jnp.float32)
    lefts = jnp.stack([in_proj, in_proj, hid_proj])
    rights = jnp.stack([gate_proj, up_proj, out_proj])
    total = jnp.einsum('ns,knr,knq->skrq', onehot, lefts, rights, precision=lax.Precision.HIGHEST)
    return total.reshape(SEQS, 3 * rank * rank)


def reference(tokens, out_grads, routes, gate_codes, w_gate, w_up, w_down, proj_in, proj_hidden):
    most = SEQS * CAP

    def one_expert(index):
        code = jnp.sum(jnp.where(routes == index, gate_codes, 0), axis=1).astype(jnp.int32)
        order = jnp.argsort(jnp.where(code > 0, 0, 1).astype(jnp.int32), stable=True)[:most].astype(jnp.int32)
        picked = code[order]
        weight = picked.astype(jnp.float32) / 4096.0
        seq_ids = jnp.where(picked > 0, order // LEN, -1).astype(jnp.int32)
        return expert_grads(tokens[order], out_grads[order], weight, seq_ids,
                            w_gate[index], w_up[index], w_down[index], proj_in, proj_hidden)

    stacked = lax.map(one_expert, jnp.arange(EXPERTS, dtype=jnp.int32))
    return jnp.transpose(stacked, (1, 0, 2))
```

```python
import jax
import jax.numpy as jnp
from jax import lax
from jax.experimental import pallas as pl
from jax.experimental.pallas import tpu as pltpu
from jax.sharding import PartitionSpec as P

CYCLE_A = (0, 1, 2, 3, 7, 4, 5, 6, 10, 11, 8, 9, 13, 14, 15, 12)
CYCLE_B = (0, 4, 8, 12, 13, 1, 5, 9, 10, 14, 2, 6, 7, 11, 15, 3)
HALF = 16
SLICES = 4
F32 = jnp.float32
BF16 = jnp.bfloat16


def place_rows(route_rows, code_rows, n_exp, cap):
    count = route_rows.shape[0]
    flat = route_rows.reshape(-1)
    pairs = flat.shape[0]
    expert_ids = jnp.arange(n_exp, dtype=jnp.int32)
    hits = (flat[:, None] == expert_ids[None, :]).astype(F32)
    earlier = (jnp.arange(pairs)[None, :] < jnp.arange(pairs)[:, None]).astype(F32)
    before = jnp.dot(earlier, hits, preferred_element_type=F32)
    place = jnp.sum(hits * before, axis=1).astype(jnp.int32)
    slot_ids = jnp.arange(cap, dtype=jnp.int32)
    match = (
        (flat[:, None, None] == expert_ids[None, :, None])
        & (place[:, None, None] == slot_ids[None, None, :])
    ).astype(jnp.int32)
    row_match = match.reshape(count, route_rows.shape[1], n_exp, cap).sum(axis=1)
    picks = row_match.reshape(count, n_exp * cap).T.astype(BF16)
    slot_code = jnp.sum(match * code_rows.reshape(-1)[:, None, None], axis=0)
    return picks, slot_code.reshape(n_exp * cap, 1).astype(F32) / 4096.0


def step_kernel(n_blocks, rows, seq_ref, *refs):
    blocks = refs[:n_blocks]
    wg, wu, wd, pin, pout, phid, pgate, pup, acc_in, acc_out, gate, upper, back, left, right = refs[n_blocks:]
    k = pl.program_id(0)
    pieces = [(b, h) for b in blocks for h in range(b.shape[0])]

    def side(which):
        return jnp.concatenate(
            [
                jnp.concatenate([b[h, j, which] for b, h in pieces], axis=0)
                for j in range(SLICES)
            ],
            axis=1,
        )

    xs = side(0)
    dys = side(1)
    terms = (
        (gate, jnp.dot(xs, wg[0], preferred_element_type=F32)),
        (upper, jnp.dot(xs, wu[0], preferred_element_type=F32)),
        (back, lax.dot_general(dys, wd[0], (((1,), (1,)), ((), ())), preferred_element_type=F32)),
        (left, jnp.dot(xs, pin[...], preferred_element_type=F32)),
        (right, jnp.dot(dys, pout[...], preferred_element_type=F32)),
    )

    @pl.when(k == 0)
    def _():
        for ref, term in terms:
            ref[...] = term

    @pl.when(k > 0)
    def _():
        for ref, term in terms:
            ref[...] += term

    @pl.when(k == pl.num_programs(0) - 1)
    def _():
        g = gate[...]
        u = upper[...]
        sig = jax.nn.sigmoid(g)
        act = g * sig
        hidden = (act * u).astype(BF16)
        b = back[...]
        d_up = (b * act).astype(BF16)
        d_gate = (b * u * sig * (1.0 + g * (1.0 - sig))).astype(BF16)
        in_hid = left[...] + jnp.dot(hidden, phid[...], preferred_element_type=F32)
        gate_up = jnp.dot(d_gate, pgate[...], preferred_element_type=F32) + jnp.dot(
            d_up, pup[...], preferred_element_type=F32
        )
        out = right[...]
        acc_out[...] = acc_in[...]
        first = 0
        for i, size in enumerate(rows):
            mine = slice(first, first + size)
            first += size
            lhs = in_hid[mine]
            tn = (((0,), (0,)), ((), ()))
            a = lax.dot_general(
                lhs, gate_up[mine], tn, precision=lax.Precision.HIGHEST, preferred_element_type=F32
            )
            c = lax.dot_general(
                lhs, out[mine], tn, precision=lax.Precision.HIGHEST, preferred_element_type=F32
            )
            total = jnp.concatenate(
                [
                    jnp.concatenate([a[0:32, 0:64], a[32:64, 0:64]], axis=1),
                    jnp.concatenate([a[0:32, 64:128], a[32:64, 64:128]], axis=1),
                    jnp.concatenate([c[64:96, 0:64], c[96:128, 0:64]], axis=1),
                ],
                axis=0,
            )
            acc_out[seq_ref[i]] += total


def step(blocks, seqs, rows, weights, acc):
    wg, wu, wd, pin, pout, phid, pgate, pup = weights
    n_rows = sum(rows)
    ff = wg.shape[2]
    depth = wg.shape[1]
    kt = SLICES * 256
    grid = depth // kt
    full = lambda a: pl.BlockSpec(a.shape, lambda k, s: (0,) * a.ndim)
    in_specs = [
        pl.BlockSpec((b.shape[0], SLICES, 2, HALF, 256), lambda k, s: (0, k, 0, 0, 0)) for b in blocks
    ] + [
        pl.BlockSpec((1, kt, ff), lambda k, s: (0, k, 0)),
        pl.BlockSpec((1, kt, ff), lambda k, s: (0, k, 0)),
        pl.BlockSpec((1, ff, kt), lambda k, s: (0, 0, k)),
        pl.BlockSpec((kt, 128), lambda k, s: (k, 0)),
        pl.BlockSpec((kt, 128), lambda k, s: (k, 0)),
        full(phid),
        full(pgate),
        full(pup),
        full(acc),
    ]
    return pl.pallas_call(
        lambda *refs: step_kernel(len(blocks), rows, *refs),
        grid_spec=pltpu.PrefetchScalarGridSpec(
            num_scalar_prefetch=1,
            grid=(grid,),
            in_specs=in_specs,
            out_specs=full(acc),
            scratch_shapes=[
                pltpu.VMEM((n_rows, ff), F32),
                pltpu.VMEM((n_rows, ff), F32),
                pltpu.VMEM((n_rows, ff), F32),
                pltpu.VMEM((n_rows, 128), F32),
                pltpu.VMEM((n_rows, 128), F32),
            ],
        ),
        out_shape=jax.ShapeDtypeStruct(acc.shape, acc.dtype),
        input_output_aliases={1 + len(blocks) + 8: 0},
        compiler_params=pltpu.CompilerParams(vmem_limit_bytes=32 * 1024 * 1024),
        cost_estimate=pl.CostEstimate(
            flops=2 * 256 * depth * ff * 3, bytes_accessed=4 * depth * ff * 3, transcendentals=n_rows * ff
        ),
        name="expert_step",
    )(seqs, *blocks, wg, wu, wd, pin, pout, phid, pgate, pup, acc)


def shift(block, cycle, way):
    n = len(cycle)
    return lax.ppermute(block, "dp", [(cycle[i], cycle[(i + way) % n]) for i in range(n)])


def even_odd(columns):
    return jnp.concatenate([columns[:, 0::2], columns[:, 1::2]], axis=1)


def per_device(tokens, out_grads, routes, gate_codes, w_gate, w_up, w_down, proj_in, proj_hidden):
    n_dp = lax.axis_size("dp")
    n_exp = lax.axis_size("expert")
    cap = tokens.shape[0] // 4
    width = tokens.shape[1]
    rank = proj_in.shape[1] // 2
    picks, weight = place_rows(routes, gate_codes, n_exp, cap)
    xs = jnp.dot(picks, tokens, preferred_element_type=F32).astype(BF16)
    dys = (jnp.dot(picks, out_grads, preferred_element_type=F32) * weight).astype(BF16)
    quarters = cap // HALF
    packed = jnp.stack(
        [xs.reshape(n_exp, quarters, HALF, width), dys.reshape(n_exp, quarters, HALF, width)], axis=2
    )
    packed = lax.all_to_all(packed, "expert", split_axis=0, concat_axis=0, tiled=True)
    packed = packed.transpose(1, 0, 2, 3, 4)
    own_a = packed[:2]
    own_b = packed[2:]

    zero = jnp.zeros((proj_in.shape[0], rank), BF16)
    pin = jnp.concatenate([even_odd(proj_in[:, :rank]), zero], axis=1)
    pout = jnp.concatenate([proj_in[:, rank:], zero], axis=1)
    zero = jnp.zeros((proj_hidden.shape[0], rank), BF16)
    phid = jnp.concatenate([zero, even_odd(proj_hidden[:, :rank])], axis=1)
    pgate = jnp.concatenate([proj_hidden[:, rank : 2 * rank], zero], axis=1)
    pup = jnp.concatenate([zero, proj_hidden[:, 2 * rank :]], axis=1)
    weights = (w_gate, w_up, w_down, pin, pout, phid, pgate, pup)

    me = lax.axis_index("dp")
    cycle_a = jnp.array(CYCLE_A, jnp.int32)
    cycle_b = jnp.array(CYCLE_B, jnp.int32)
    at_a = jnp.argmax(cycle_a == me).astype(jnp.int32)
    at_b = jnp.argmax(cycle_b == me).astype(jnp.int32)
    hops = jnp.arange(n_dp // 2 + 1, dtype=jnp.int32)
    seqs = jnp.stack(
        [
            cycle_a[(at_a - hops) % n_dp],
            cycle_a[(at_a + hops) % n_dp],
            cycle_b[(at_b - hops) % n_dp],
            cycle_b[(at_b + hops) % n_dp],
        ],
        axis=1,
    )

    acc = jnp.zeros((n_dp, 3 * rank * rank // 128, 128), F32)
    ap, am, bp, bm = own_a, own_a, own_b, own_b
    last = n_dp // 2
    for hop in range(last + 1):
        if hop < last - 1:
            sent = (ap, am, bp, bm)
        else:
            sent = (ap[:1], am[1:], bp[:1], bm[1:])
        if hop < last:
            after = (
                shift(sent[0], CYCLE_A, 1),
                shift(sent[1], CYCLE_A, -1),
                shift(sent[2], CYCLE_B, 1),
                shift(sent[3], CYCLE_B, -1),
            )
        if hop == 0:
            acc = step([own_a, own_b], seqs[0, 1:3], (32, 32), weights, acc)
        elif hop < last:
            acc = step([ap, am, bp, bm], seqs[hop], (32, 32, 32, 32), weights, acc)
        else:
            acc = step([ap, am, bp, bm], seqs[hop, 1:3], (32, 32), weights, acc)
        if hop < last:
            ap, am, bp, bm = after

    share = acc.reshape(n_dp, n_dp, -1, 128).transpose(1, 2, 0, 3)
    share = lax.all_to_all(share, "dp", split_axis=0, concat_axis=0, tiled=True)
    total = jnp.sum(share, axis=0)
    return total.transpose(1, 0, 2).reshape(n_dp, 1, -1)


def solution(mesh):
    return jax.shard_map(
        per_device,
        mesh=mesh,
        in_specs=(
            P("dp", "expert"),
            P("dp", "expert"),
            P("dp", None),
            P("dp", None),
            P("expert", None, "dp"),
            P("expert", None, "dp"),
            P("expert", "dp", None),
            P(),
            P("dp", None),
        ),
        out_specs=P(None, "expert", "dp"),
        check_vma=False,
    )
```

```python
import jax
import jax.numpy as jnp
from jax import lax
from jax.experimental import pallas as pl
from jax.experimental.pallas import tpu as pltpu
from jax.sharding import PartitionSpec as P

SIDE = 4
ROWS = 16
LANES = 128
DEPTH = 1024
F32 = jnp.float32
BF16 = jnp.bfloat16


def place_rows(route_rows, code_rows, n_exp, cap, mine):
    count = route_rows.shape[0]
    flat = route_rows.reshape(-1)
    pairs = flat.shape[0]
    expert_ids = jnp.arange(n_exp, dtype=jnp.int32)
    hits = (flat[:, None] == expert_ids[None, :]).astype(F32)
    earlier = (jnp.arange(pairs)[None, :] < jnp.arange(pairs)[:, None]).astype(F32)
    before = jnp.dot(earlier, hits, preferred_element_type=F32)
    place = jnp.sum(hits * before, axis=1).astype(jnp.int32)
    slot = jnp.arange(n_exp * cap, dtype=jnp.int32)
    target = (flat * cap + place).reshape(count, -1)
    picks = (slot[:, None] == target[:, 0][None, :]) | (slot[:, None] == target[:, 1][None, :])
    own = mine * cap + jnp.arange(cap, dtype=jnp.int32)
    codes = jnp.sum(
        jnp.where(own[:, None] == target.reshape(-1)[None, :], code_rows.reshape(-1)[None, :], 0), axis=1
    )
    return picks.astype(BF16), codes


def dot_t(rows, columns):
    return lax.dot_general(rows, columns, (((1,), (1,)), ((), ())), preferred_element_type=F32)


def step_kernel(sources, n_bufs, first, me_ref, *refs):
    rest = refs[3 * n_bufs :]
    wg, wu, wd, pin, phid = rest[:5]
    acc_in = None if first else rest[5]
    acc_out, gate, upper, back, left, right, turn = rest[5 if first else 6 :]
    k = pl.program_id(0)

    def side(which):
        parts = [refs[3 * i + which][s : s + c] for _, parts in sources for i, s, c in parts]
        return jnp.concatenate([p.reshape(p.shape[0] * ROWS, p.shape[2]) for p in parts], axis=0)

    xs = side(0)
    dys = side(1)
    terms = (
        (gate, lambda: dot_t(xs, wg[0])),
        (upper, lambda: dot_t(xs, wu[0])),
        (back, lambda: dot_t(dys, wd[0])),
        (left, lambda: jnp.dot(xs, pin[...], preferred_element_type=F32)),
        (right, lambda: jnp.dot(dys, pin[...], preferred_element_type=F32)),
    )

    @pl.when(k == 0)
    def _():
        for ref, term in terms:
            ref[...] = term()

    @pl.when(k > 0)
    def _():
        for ref, term in terms:
            ref[...] += term()

    @pl.when(k == pl.num_programs(0) - 1)
    def _():
        codes = side(2).astype(F32)
        weight = (codes[:, 0:1] * 16.0 + codes[:, 1:2]) / 4096.0
        g = gate[...]
        u = upper[...]
        sig = jax.nn.sigmoid(g)
        act = g * sig
        hidden = (act * u).astype(BF16)
        b = back[...] * weight
        d_up = (b * act).astype(BF16)
        d_gate = (b * u * sig * (1.0 + g * (1.0 - sig))).astype(BF16)
        hid = dot_t(hidden, phid[...])
        dgp = dot_t(d_gate, phid[...])
        dup = dot_t(d_up, phid[...])
        gate_up = jnp.concatenate([dgp[:, 64:128], dup[:, 128:192]], axis=1)
        out = right[...] * weight
        ins = left[...]
        acc_out[...] = jnp.zeros(acc_out.shape, F32) if first else acc_in[...]
        me = me_ref[0]
        row = 0
        tn = (((0,), (0,)), ((), ()))
        for i, (offset, parts) in enumerate(sources):
            size = ROWS * sum(c for _, _, c in parts)
            mine = slice(row, row + size)
            row += size
            a = lax.dot_general(
                ins[mine, :64], gate_up[mine], tn, precision=lax.Precision.HIGHEST, preferred_element_type=F32
            )
            c = lax.dot_general(
                hid[mine, :64], out[mine], tn, precision=lax.Precision.HIGHEST, preferred_element_type=F32
            )
            turn[i, 0:64] = a
            turn[i, 64:128] = c
            even_a = turn[i, pl.ds(0, 32, stride=2)]
            odd_a = turn[i, pl.ds(1, 32, stride=2)]
            even_c = turn[i, pl.ds(64, 32, stride=2)]
            odd_c = turn[i, pl.ds(65, 32, stride=2)]
            total = jnp.concatenate(
                [
                    jnp.concatenate([even_a[:, :64], odd_a[:, :64]], axis=1),
                    jnp.concatenate([even_a[:, 64:], odd_a[:, 64:]], axis=1),
                    jnp.concatenate([even_c[:, 64:], odd_c[:, 64:]], axis=1),
                ],
                axis=0,
            )
            x_at = lax.rem(lax.rem(me, SIDE) - offset[0] + SIDE, SIDE)
            y_at = lax.rem(lax.div(me, SIDE) - offset[1] + SIDE, SIDE)
            acc_out[y_at * SIDE + x_at] += total


def step(blocks, me, weights, acc, acc_shape):
    wg, wu, wd, pin, phid = weights
    bufs, sources = [], []

    def index(buf):
        for i, other in enumerate(bufs):
            if other is buf:
                return i
        bufs.append(buf)
        return len(bufs) - 1

    for offset, parts in blocks.items():
        sources.append((offset, [(index(b), s, c) for b, s, c in parts]))
    n_rows = ROWS * sum(c for s in sources for _, _, c in s[1])
    ff = wg.shape[1]
    depth = wg.shape[2]
    full = lambda shape: pl.BlockSpec(shape, lambda k, s: (0,) * len(shape))
    in_specs = []
    for b in bufs:
        in_specs += [
            pl.BlockSpec((b.shape[0], ROWS, DEPTH), lambda k, s: (0, 0, k)),
            pl.BlockSpec((b.shape[0], ROWS, DEPTH), lambda k, s: (0, 0, k + depth // DEPTH)),
            pl.BlockSpec((b.shape[0], ROWS, LANES), lambda k, s: (0, 0, 2 * depth // LANES)),
        ]
    in_specs += [
        pl.BlockSpec((1, ff, DEPTH), lambda k, s: (0, 0, k)),
        pl.BlockSpec((1, ff, DEPTH), lambda k, s: (0, 0, k)),
        pl.BlockSpec((1, ff, DEPTH), lambda k, s: (0, 0, k)),
        pl.BlockSpec((DEPTH, 128), lambda k, s: (k, 0)),
        full(phid.shape),
    ]
    args = [me] + [b for b in bufs for _ in range(3)] + [wg, wu, wd, pin, phid]
    first = acc is None
    aliases = {}
    if not first:
        aliases = {len(args): 0}
        args.append(acc)
        in_specs.append(full(acc_shape))
    return pl.pallas_call(
        lambda *refs: step_kernel(sources, len(bufs), first, *refs),
        grid_spec=pltpu.PrefetchScalarGridSpec(
            num_scalar_prefetch=1,
            grid=(depth // DEPTH,),
            in_specs=in_specs,
            out_specs=full(acc_shape),
            scratch_shapes=[
                pltpu.VMEM((n_rows, ff), F32),
                pltpu.VMEM((n_rows, ff), F32),
                pltpu.VMEM((n_rows, ff), F32),
                pltpu.VMEM((n_rows, 128), F32),
                pltpu.VMEM((n_rows, 128), F32),
                pltpu.VMEM((len(sources), 128, 128), F32),
            ],
        ),
        out_shape=jax.ShapeDtypeStruct(acc_shape, F32),
        input_output_aliases=aliases,
        compiler_params=pltpu.CompilerParams(vmem_limit_bytes=32 * 1024 * 1024),
        cost_estimate=pl.CostEstimate(
            flops=2 * n_rows * depth * ff * 3, bytes_accessed=2 * depth * ff * 3, transcendentals=n_rows * ff
        ),
        name="expert_step",
    )(*args)


def shift(block, axis, way):
    moves = []
    for y in range(SIDE):
        for x in range(SIDE):
            to = (y, (x + way) % SIDE) if axis == 0 else ((y + way) % SIDE, x)
            moves.append((y * SIDE + x, to[0] * SIDE + to[1]))
    return lax.ppermute(block, "dp", moves)


def per_device(tokens, out_grads, routes, gate_codes, w_gate, w_up, w_down, proj_in, proj_hidden):
    n_dp = lax.axis_size("dp")
    n_exp = lax.axis_size("expert")
    cap = tokens.shape[0] // 4
    width = tokens.shape[1]
    rank = proj_in.shape[1] // 2
    me = lax.axis_index("dp").astype(jnp.int32).reshape(1)
    picks, codes = place_rows(routes, gate_codes, n_exp, cap, lax.axis_index("expert"))
    both = jnp.concatenate([tokens, out_grads], axis=1)
    slots = jnp.dot(picks, both, preferred_element_type=F32).astype(BF16)
    pieces = cap // ROWS
    slots = slots.reshape(n_exp, pieces, ROWS, 2, width)
    slots = lax.all_to_all(slots, "expert", split_axis=0, concat_axis=0, tiled=True)
    codes = codes.reshape(pieces, ROWS, 1)
    lane = jnp.arange(LANES, dtype=jnp.int32)
    meta = jnp.where(lane == 0, codes // 16, jnp.where(lane == 1, codes % 16, 0)).astype(BF16)
    own = slots.transpose(1, 2, 3, 0, 4).reshape(pieces, ROWS, 2 * n_exp * width)
    own = jnp.concatenate([own, meta], axis=2)

    weights = (w_gate.transpose(0, 2, 1), w_up.transpose(0, 2, 1), w_down, proj_in, proj_hidden.T)
    acc_shape = (n_dp, 3 * rank * rank // LANES, LANES)
    half = pieces // 2
    whole = lambda buf: [(buf, 0, pieces)]
    run = lambda blocks, acc: step(blocks, me, weights, acc, acc_shape)
    b10, b30, b01, b03 = shift(own, 0, 1), shift(own, 0, -1), shift(own, 1, 1), shift(own, 1, -1)
    b11, b33, b13, b31 = shift(b10, 1, 1), shift(b30, 1, -1), shift(b03, 0, 1), shift(b01, 0, -1)
    acc = run(
        {(0, 0): whole(own), (1, 0): whole(b10), (3, 0): whole(b30), (0, 1): whole(b01), (0, 3): whole(b03)}, None
    )
    b11, b33, b13, b31, acc = lax.optimization_barrier((b11, b33, b13, b31, acc))
    b21, b23, b12, b32 = shift(b11, 0, 1), shift(b33, 0, -1), shift(b13, 1, -1), shift(b31, 1, 1)
    acc = run({(1, 1): whole(b11), (3, 3): whole(b33), (1, 3): whole(b13), (3, 1): whole(b31)}, acc)
    b21, b23, b12, b32, acc = lax.optimization_barrier((b21, b23, b12, b32, acc))
    cat = lambda *parts: jnp.concatenate(parts, axis=0)
    east, west = shift(cat(b10[:half], b12[0:1]), 0, 1), shift(cat(b30[half:], b32[1:2]), 0, -1)
    north, south = shift(cat(b01[:half], b21[2:3]), 1, 1), shift(cat(b03[half:], b23[3:4]), 1, -1)
    acc = run({(2, 1): whole(b21), (2, 3): whole(b23), (1, 2): whole(b12), (3, 2): whole(b32)}, acc)
    acc = run(
        {
            (2, 0): [(east, 0, half), (west, 0, half)],
            (0, 2): [(north, 0, half), (south, 0, half)],
            (2, 2): [(q, half, 1) for q in (east, west, north, south)],
        },
        acc,
    )

    share = acc.reshape(n_dp, n_dp, -1, LANES).transpose(1, 2, 0, 3)
    share = lax.all_to_all(share, "dp", split_axis=0, concat_axis=0, tiled=True)
    total = jnp.sum(share, axis=0)
    return total.transpose(1, 0, 2).reshape(n_dp, 1, -1)


def solution(mesh):
    return jax.shard_map(
        per_device,
        mesh=mesh,
        in_specs=(
            P("dp", "expert"),
            P("dp", "expert"),
            P("dp", None),
            P("dp", None),
            P("expert", None, "dp"),
            P("expert", None, "dp"),
            P("expert", "dp", None),
            P(),
            P("dp", None),
        ),
        out_specs=P(None, "expert", "dp"),
        check_vma=False,
    )
```

```python
import jax
import jax.numpy as jnp
from jax import lax
from jax.experimental import pallas as pl
from jax.experimental.pallas import tpu as pltpu
from jax.sharding import PartitionSpec as P

SIDE = 4
ROWS = 16
LANES = 128
DEPTH = 1024
F32 = jnp.float32
BF16 = jnp.bfloat16


def pack_kernel(cap, mine_ref, routes_ref, codes_ref, tokens_ref, grads_ref, slots_ref, meta_ref):
    n_exp = slots_ref.shape[0]
    count = tokens_ref.shape[0]
    shape = (n_exp, count)
    expert = lax.broadcasted_iota(jnp.int32, shape, 0)
    hits = jnp.where(routes_ref[0:1] == expert, 1.0, 0.0) + jnp.where(routes_ref[1:2] == expert, 1.0, 0.0)
    earlier = lax.broadcasted_iota(jnp.int32, (count, count), 0) < lax.broadcasted_iota(jnp.int32, (count, count), 1)
    before = jnp.dot(hits.astype(BF16), jnp.where(earlier, 1.0, 0.0).astype(BF16), preferred_element_type=F32)
    place = jnp.where(hits > 0.0, before, -1.0)
    slot = lax.broadcasted_iota(jnp.int32, (cap, count), 0).astype(F32)
    values = jnp.concatenate([tokens_ref[...], grads_ref[...]], axis=1)
    width = tokens_ref.shape[1]
    for e in range(n_exp):
        picks = jnp.where(place[e : e + 1] == slot, 1.0, 0.0).astype(BF16)
        rows = jnp.dot(picks, values, preferred_element_type=F32).astype(BF16)
        slots_ref[e, 0] = rows[:, :width].reshape(cap // ROWS, ROWS, width)
        slots_ref[e, 1] = rows[:, width:].reshape(cap // ROWS, ROWS, width)
    mine = mine_ref[0]
    here = jnp.sum(jnp.where(expert == mine, place, 0.0), axis=0, keepdims=True)
    named = jnp.where(routes_ref[0:1] == mine, codes_ref[0:1], 0) + jnp.where(
        routes_ref[1:2] == mine, codes_ref[1:2], 0
    )
    codes = jnp.sum(jnp.where(here == slot, named, 0).astype(F32), axis=1, keepdims=True)
    high = jnp.floor(codes * (1.0 / 16.0))
    lane = lax.broadcasted_iota(jnp.int32, (cap, LANES), 1)
    meta = jnp.where(lane == 0, high, jnp.where(lane == 1, codes - 16.0 * high, 0.0))
    meta_ref[...] = meta.astype(BF16).reshape(cap // ROWS, ROWS, LANES)


def lay_kernel(slots_ref, meta_ref, own_ref):
    n_exp, sides, _, _, width = slots_ref.shape
    for w in range(sides):
        for d in range(n_exp):
            at = (w * n_exp + d) * width
            own_ref[:, :, at : at + width] = slots_ref[d, w]
    own_ref[:, :, sides * n_exp * width :] = meta_ref[...]


def dot_t(rows, columns):
    return lax.dot_general(rows, columns, (((1,), (1,)), ((), ())), preferred_element_type=F32)


def step_kernel(sources, n_bufs, first, me_ref, *refs):
    bufs = refs[:n_bufs]
    wg, wu, wd, pin, phid = refs[n_bufs : n_bufs + 5]
    rest = refs[n_bufs + 5 :]
    acc_in = None if first else rest[0]
    acc_out, gate, upper, back, left, right, turn = rest[0 if first else 1 :]
    depth = wg.shape[2]

    def side(start, size):
        parts = [bufs[i][s : s + c, :, start : start + size] for _, parts in sources for i, s, c in parts]
        return jnp.concatenate([p.reshape(p.shape[0] * ROWS, size) for p in parts], axis=0)

    for at in range(0, depth, DEPTH):
        part = slice(at, at + DEPTH)
        xs = side(at, DEPTH)
        dys = side(depth + at, DEPTH)
        for ref, term in (
            (gate, dot_t(xs, wg[0, :, part])),
            (upper, dot_t(xs, wu[0, :, part])),
            (back, dot_t(dys, wd[0, :, part])),
            (left, jnp.dot(xs, pin[part], preferred_element_type=F32)),
            (right, jnp.dot(dys, pin[part], preferred_element_type=F32)),
        ):
            ref[...] = term if at == 0 else ref[...] + term

    codes = side(2 * depth, LANES).astype(F32)
    weight = (codes[:, 0:1] * 16.0 + codes[:, 1:2]) / 4096.0
    g = gate[...]
    u = upper[...]
    sig = jax.nn.sigmoid(g)
    act = g * sig
    hidden = (act * u).astype(BF16)
    b = back[...] * weight
    d_up = (b * act).astype(BF16)
    d_gate = (b * u * sig * (1.0 + g * (1.0 - sig))).astype(BF16)
    hid = dot_t(hidden, phid[...])
    dgp = dot_t(d_gate, phid[...])
    dup = dot_t(d_up, phid[...])
    gate_up = jnp.concatenate([dgp[:, 64:128], dup[:, 128:192]], axis=1)
    out = right[...] * weight
    ins = left[...]
    acc_out[...] = jnp.zeros(acc_out.shape, F32) if first else acc_in[...]
    me = me_ref[0]
    row = 0
    tn = (((0,), (0,)), ((), ()))
    for i, (offset, parts) in enumerate(sources):
        size = ROWS * sum(c for _, _, c in parts)
        mine = slice(row, row + size)
        row += size
        a = lax.dot_general(
            ins[mine, :64], gate_up[mine], tn, precision=lax.Precision.HIGHEST, preferred_element_type=F32
        )
        c = lax.dot_general(
            hid[mine, :64], out[mine], tn, precision=lax.Precision.HIGHEST, preferred_element_type=F32
        )
        turn[i, 0:64] = a
        turn[i, 64:128] = c
        even_a = turn[i, pl.ds(0, 32, stride=2)]
        odd_a = turn[i, pl.ds(1, 32, stride=2)]
        even_c = turn[i, pl.ds(64, 32, stride=2)]
        odd_c = turn[i, pl.ds(65, 32, stride=2)]
        total = jnp.concatenate(
            [
                jnp.concatenate([even_a[:, :64], odd_a[:, :64]], axis=1),
                jnp.concatenate([even_a[:, 64:], odd_a[:, 64:]], axis=1),
                jnp.concatenate([even_c[:, 64:], odd_c[:, 64:]], axis=1),
            ],
            axis=0,
        )
        x_at = lax.rem(lax.rem(me, SIDE) - offset[0] + SIDE, SIDE)
        y_at = lax.rem(lax.div(me, SIDE) - offset[1] + SIDE, SIDE)
        acc_out[y_at * SIDE + x_at] += total


def step(blocks, me, weights, acc, acc_shape):
    wg, wu, wd, pin, phid = weights
    bufs, sources = [], []

    def index(buf):
        for i, other in enumerate(bufs):
            if other is buf:
                return i
        bufs.append(buf)
        return len(bufs) - 1

    for offset, parts in blocks.items():
        sources.append((offset, [(index(b), s, c) for b, s, c in parts]))
    n_rows = ROWS * sum(c for s in sources for _, _, c in s[1])
    ff = wg.shape[1]
    depth = wg.shape[2]
    args = [me, *bufs, wg, wu, wd, pin, phid]
    first = acc is None
    aliases = {}
    if not first:
        aliases = {len(args): 0}
        args.append(acc)
    return pl.pallas_call(
        lambda *refs: step_kernel(sources, len(bufs), first, *refs),
        in_specs=[pl.BlockSpec(memory_space=pltpu.SMEM)] + [pl.BlockSpec(memory_space=pltpu.VMEM)] * (len(args) - 1),
        out_specs=pl.BlockSpec(memory_space=pltpu.VMEM),
        scratch_shapes=[
            pltpu.VMEM((n_rows, ff), F32),
            pltpu.VMEM((n_rows, ff), F32),
            pltpu.VMEM((n_rows, ff), F32),
            pltpu.VMEM((n_rows, 128), F32),
            pltpu.VMEM((n_rows, 128), F32),
            pltpu.VMEM((len(sources), 128, 128), F32),
        ],
        out_shape=jax.ShapeDtypeStruct(acc_shape, F32),
        input_output_aliases=aliases,
        compiler_params=pltpu.CompilerParams(vmem_limit_bytes=32 * 1024 * 1024),
        cost_estimate=pl.CostEstimate(
            flops=2 * n_rows * depth * ff * 3, bytes_accessed=2 * depth * ff * 3, transcendentals=n_rows * ff
        ),
        name="expert_step",
    )(*args)


def shift(block, axis, way):
    moves = []
    for y in range(SIDE):
        for x in range(SIDE):
            to = (y, (x + way) % SIDE) if axis == 0 else ((y + way) % SIDE, x)
            moves.append((y * SIDE + x, to[0] * SIDE + to[1]))
    return lax.ppermute(block, "dp", moves)


def after(acc, *bufs):
    held = []
    for buf in bufs:
        buf, acc = lax.optimization_barrier((buf, acc))
        held.append(buf)
    return (*held, acc)


def per_device(tokens, out_grads, routes, gate_codes, w_gate, w_up, w_down, proj_in, proj_hidden):
    n_dp = lax.axis_size("dp")
    n_exp = lax.axis_size("expert")
    cap = tokens.shape[0] // 4
    width = tokens.shape[1]
    rank = proj_in.shape[1] // 2
    me = lax.axis_index("dp").astype(jnp.int32).reshape(1)
    mine = lax.axis_index("expert").astype(jnp.int32).reshape(1)
    pieces = cap // ROWS
    vmem = pl.BlockSpec(memory_space=pltpu.VMEM)
    slots, meta = pl.pallas_call(
        lambda *refs: pack_kernel(cap, *refs),
        in_specs=[pl.BlockSpec(memory_space=pltpu.SMEM), vmem, vmem, vmem, vmem],
        out_specs=[vmem, vmem],
        out_shape=[
            jax.ShapeDtypeStruct((n_exp, 2, pieces, ROWS, width), BF16),
            jax.ShapeDtypeStruct((pieces, ROWS, LANES), BF16),
        ],
        name="pack_slots",
    )(mine, routes.T, gate_codes.T, tokens, out_grads)
    slots = lax.all_to_all(slots, "expert", split_axis=0, concat_axis=0, tiled=True)
    own = pl.pallas_call(
        lay_kernel,
        in_specs=[vmem, vmem],
        out_specs=vmem,
        out_shape=jax.ShapeDtypeStruct((pieces, ROWS, 2 * n_exp * width + LANES), BF16),
        name="lay_rows",
    )(slots, meta)

    weights = (w_gate.transpose(0, 2, 1), w_up.transpose(0, 2, 1), w_down, proj_in, proj_hidden.T)
    acc_shape = (n_dp, 3 * rank * rank // LANES, LANES)
    half = pieces // 2
    whole = lambda buf: [(buf, 0, pieces)]
    run = lambda blocks, acc: step(blocks, me, weights, acc, acc_shape)
    b10, b30, b01, b03 = shift(own, 0, 1), shift(own, 0, -1), shift(own, 1, 1), shift(own, 1, -1)
    b11, b33, b13, b31 = shift(b10, 1, 1), shift(b30, 1, -1), shift(b03, 0, 1), shift(b01, 0, -1)
    acc = run(
        {(0, 0): whole(own), (1, 0): whole(b10), (3, 0): whole(b30), (0, 1): whole(b01), (0, 3): whole(b03)}, None
    )
    b11, b33, b13, b31, acc = after(acc, b11, b33, b13, b31)
    b21, b23, b12, b32 = shift(b11, 0, 1), shift(b33, 0, -1), shift(b13, 1, -1), shift(b31, 1, 1)
    acc = run({(1, 1): whole(b11), (3, 3): whole(b33), (1, 3): whole(b13), (3, 1): whole(b31)}, acc)
    b21, b23, b12, b32, acc = after(acc, b21, b23, b12, b32)
    cat = lambda *parts: jnp.concatenate(parts, axis=0)
    east, west = shift(cat(b10[:half], b12[0:1]), 0, 1), shift(cat(b30[half:], b32[1:2]), 0, -1)
    north, south = shift(cat(b01[:half], b21[2:3]), 1, 1), shift(cat(b03[half:], b23[3:4]), 1, -1)
    acc = run({(2, 1): whole(b21), (2, 3): whole(b23), (1, 2): whole(b12), (3, 2): whole(b32)}, acc)
    acc = run(
        {
            (2, 0): [(east, 0, half), (west, 0, half)],
            (0, 2): [(north, 0, half), (south, 0, half)],
            (2, 2): [(q, half, 1) for q in (east, west, north, south)],
        },
        acc,
    )

    share = acc.reshape(n_dp, n_dp, -1, LANES).transpose(1, 2, 0, 3)
    share = lax.all_to_all(share, "dp", split_axis=0, concat_axis=0, tiled=True)
    total = jnp.sum(share, axis=0)
    return total.transpose(1, 0, 2).reshape(n_dp, 1, -1)


def solution(mesh):
    return jax.shard_map(
        per_device,
        mesh=mesh,
        in_specs=(
            P("dp", "expert"),
            P("dp", "expert"),
            P("dp", None),
            P("dp", None),
            P("expert", None, "dp"),
            P("expert", None, "dp"),
            P("expert", "dp", None),
            P(),
            P("dp", None),
        ),
        out_specs=P(None, "expert", "dp"),
        check_vma=False,
    )
```

```python
import jax
import jax.numpy as jnp
from jax import lax
from jax.experimental import pallas as pl
from jax.experimental.pallas import tpu as pltpu
from jax.sharding import PartitionSpec as P

SIDE = 4
ROWS = 16
LANES = 128
DEPTH = 1024
F32 = jnp.float32
BF16 = jnp.bfloat16


def pack_kernel(cap, mine_ref, routes_ref, codes_ref, tokens_ref, grads_ref, slots_ref, meta_ref):
    n_exp = slots_ref.shape[0]
    count = tokens_ref.shape[0]
    shape = (n_exp, count)
    expert = lax.broadcasted_iota(jnp.int32, shape, 0)
    hits = jnp.where(routes_ref[0:1] == expert, 1.0, 0.0) + jnp.where(routes_ref[1:2] == expert, 1.0, 0.0)
    earlier = lax.broadcasted_iota(jnp.int32, (count, count), 0) < lax.broadcasted_iota(jnp.int32, (count, count), 1)
    before = jnp.dot(hits.astype(BF16), jnp.where(earlier, 1.0, 0.0).astype(BF16), preferred_element_type=F32)
    place = jnp.where(hits > 0.0, before, -1.0)
    slot = lax.broadcasted_iota(jnp.int32, (cap, count), 0).astype(F32)
    values = jnp.concatenate([tokens_ref[...], grads_ref[...]], axis=1)
    width = tokens_ref.shape[1]
    for e in range(n_exp):
        picks = jnp.where(place[e : e + 1] == slot, 1.0, 0.0).astype(BF16)
        rows = jnp.dot(picks, values, preferred_element_type=F32).astype(BF16)
        slots_ref[e, 0] = rows[:, :width].reshape(cap // ROWS, ROWS, width)
        slots_ref[e, 1] = rows[:, width:].reshape(cap // ROWS, ROWS, width)
    mine = mine_ref[0]
    here = jnp.sum(jnp.where(expert == mine, place, 0.0), axis=0, keepdims=True)
    named = jnp.where(routes_ref[0:1] == mine, codes_ref[0:1], 0) + jnp.where(
        routes_ref[1:2] == mine, codes_ref[1:2], 0
    )
    codes = jnp.sum(jnp.where(here == slot, named, 0).astype(F32), axis=1, keepdims=True)
    high = jnp.floor(codes * (1.0 / 16.0))
    lane = lax.broadcasted_iota(jnp.int32, (cap, LANES), 1)
    meta = jnp.where(lane == 0, high, jnp.where(lane == 1, codes - 16.0 * high, 0.0))
    meta_ref[...] = meta.astype(BF16).reshape(cap // ROWS, ROWS, LANES)


def lay_kernel(slots_ref, meta_ref, own_ref):
    n_exp, sides, _, _, width = slots_ref.shape
    for w in range(sides):
        for d in range(n_exp):
            at = (w * n_exp + d) * width
            own_ref[:, :, at : at + width] = slots_ref[d, w]
    own_ref[:, :, sides * n_exp * width :] = meta_ref[...]


def dot_t(rows, columns):
    return lax.dot_general(rows, columns, (((1,), (1,)), ((), ())), preferred_element_type=F32)


def step_kernel(sources, n_bufs, first, me_ref, *refs):
    bufs = refs[:n_bufs]
    wg, wu, wd, pin, phid = refs[n_bufs : n_bufs + 5]
    rest = refs[n_bufs + 5 :]
    acc_in = None if first else rest[0]
    acc_out, gate, upper, back, left, right, turn = rest[0 if first else 1 :]
    depth = wg.shape[2]

    def side(start, size):
        parts = [bufs[i][s : s + c, :, start : start + size] for _, parts in sources for i, s, c in parts]
        return jnp.concatenate([p.reshape(p.shape[0] * ROWS, size) for p in parts], axis=0)

    for at in range(0, depth, DEPTH):
        part = slice(at, at + DEPTH)
        xs = side(at, DEPTH)
        dys = side(depth + at, DEPTH)
        for ref, term in (
            (gate, dot_t(xs, wg[0, :, part])),
            (upper, dot_t(xs, wu[0, :, part])),
            (back, dot_t(dys, wd[0, :, part])),
            (left, jnp.dot(xs, pin[part], preferred_element_type=F32)),
            (right, jnp.dot(dys, pin[part], preferred_element_type=F32)),
        ):
            ref[...] = term if at == 0 else ref[...] + term

    codes = side(2 * depth, LANES).astype(F32)
    weight = (codes[:, 0:1] * 16.0 + codes[:, 1:2]) / 4096.0
    g = gate[...]
    u = upper[...]
    sig = jax.nn.sigmoid(g)
    act = g * sig
    hidden = (act * u).astype(BF16)
    b = back[...] * weight
    d_up = (b * act).astype(BF16)
    d_gate = (b * u * sig * (1.0 + g * (1.0 - sig))).astype(BF16)
    hid = dot_t(hidden, phid[...])
    dgp = dot_t(d_gate, phid[...])
    dup = dot_t(d_up, phid[...])
    gate_up = jnp.concatenate([dgp[:, 64:128], dup[:, 128:192]], axis=1)
    out = right[...] * weight
    ins = left[...]
    acc_out[...] = jnp.zeros(acc_out.shape, F32) if first else acc_in[...]
    me = me_ref[0]
    row = 0
    tn = (((0,), (0,)), ((), ()))
    for i, (offset, parts) in enumerate(sources):
        size = ROWS * sum(c for _, _, c in parts)
        mine = slice(row, row + size)
        row += size
        a = lax.dot_general(
            ins[mine, :64], gate_up[mine], tn, precision=lax.Precision.HIGHEST, preferred_element_type=F32
        )
        c = lax.dot_general(
            hid[mine, :64], out[mine], tn, precision=lax.Precision.HIGHEST, preferred_element_type=F32
        )
        turn[i, 0:64] = a
        turn[i, 64:128] = c
        even_a = turn[i, pl.ds(0, 32, stride=2)]
        odd_a = turn[i, pl.ds(1, 32, stride=2)]
        even_c = turn[i, pl.ds(64, 32, stride=2)]
        odd_c = turn[i, pl.ds(65, 32, stride=2)]
        total = jnp.concatenate(
            [
                jnp.concatenate([even_a[:, :64], odd_a[:, :64]], axis=1),
                jnp.concatenate([even_a[:, 64:], odd_a[:, 64:]], axis=1),
                jnp.concatenate([even_c[:, 64:], odd_c[:, 64:]], axis=1),
            ],
            axis=0,
        )
        x_at = lax.rem(lax.rem(me, SIDE) - offset[0] + SIDE, SIDE)
        y_at = lax.rem(lax.div(me, SIDE) - offset[1] + SIDE, SIDE)
        acc_out[y_at * SIDE + x_at] += total


def step(blocks, me, weights, acc, acc_shape):
    wg, wu, wd, pin, phid = weights
    bufs, sources = [], []

    def index(buf):
        for i, other in enumerate(bufs):
            if other is buf:
                return i
        bufs.append(buf)
        return len(bufs) - 1

    for offset, parts in blocks.items():
        sources.append((offset, [(index(b), s, c) for b, s, c in parts]))
    n_rows = ROWS * sum(c for s in sources for _, _, c in s[1])
    ff = wg.shape[1]
    depth = wg.shape[2]
    args = [me, *bufs, wg, wu, wd, pin, phid]
    first = acc is None
    aliases = {}
    if not first:
        aliases = {len(args): 0}
        args.append(acc)
    return pl.pallas_call(
        lambda *refs: step_kernel(sources, len(bufs), first, *refs),
        in_specs=[pl.BlockSpec(memory_space=pltpu.SMEM)] + [pl.BlockSpec(memory_space=pltpu.VMEM)] * (len(args) - 1),
        out_specs=pl.BlockSpec(memory_space=pltpu.VMEM),
        scratch_shapes=[
            pltpu.VMEM((n_rows, ff), F32),
            pltpu.VMEM((n_rows, ff), F32),
            pltpu.VMEM((n_rows, ff), F32),
            pltpu.VMEM((n_rows, 128), F32),
            pltpu.VMEM((n_rows, 128), F32),
            pltpu.VMEM((len(sources), 128, 128), F32),
        ],
        out_shape=jax.ShapeDtypeStruct(acc_shape, F32),
        input_output_aliases=aliases,
        compiler_params=pltpu.CompilerParams(vmem_limit_bytes=32 * 1024 * 1024),
        cost_estimate=pl.CostEstimate(
            flops=2 * n_rows * depth * ff * 3, bytes_accessed=2 * depth * ff * 3, transcendentals=n_rows * ff
        ),
        name="expert_step",
    )(*args)


def shift(block, axis, way):
    moves = []
    for y in range(SIDE):
        for x in range(SIDE):
            to = (y, (x + way) % SIDE) if axis == 0 else ((y + way) % SIDE, x)
            moves.append((y * SIDE + x, to[0] * SIDE + to[1]))
    return lax.ppermute(block, "dp", moves)


def after(acc, *bufs):
    held = []
    for buf in bufs:
        buf, acc = lax.optimization_barrier((buf, acc))
        held.append(buf)
    return (*held, acc)


def per_device(tokens, out_grads, routes, gate_codes, w_gate, w_up, w_down, proj_in, proj_hidden):
    n_dp = lax.axis_size("dp")
    n_exp = lax.axis_size("expert")
    cap = tokens.shape[0] // 4
    width = tokens.shape[1]
    rank = proj_in.shape[1] // 2
    me = lax.axis_index("dp").astype(jnp.int32).reshape(1)
    mine = lax.axis_index("expert").astype(jnp.int32).reshape(1)
    pieces = cap // ROWS
    vmem = pl.BlockSpec(memory_space=pltpu.VMEM)
    slots, meta = pl.pallas_call(
        lambda *refs: pack_kernel(cap, *refs),
        in_specs=[pl.BlockSpec(memory_space=pltpu.SMEM), vmem, vmem, vmem, vmem],
        out_specs=[vmem, vmem],
        out_shape=[
            jax.ShapeDtypeStruct((n_exp, 2, pieces, ROWS, width), BF16),
            jax.ShapeDtypeStruct((pieces, ROWS, LANES), BF16),
        ],
        name="pack_slots",
    )(mine, routes.T, gate_codes.T, tokens, out_grads)
    slots = lax.all_to_all(slots, "expert", split_axis=0, concat_axis=0, tiled=True)
    own = pl.pallas_call(
        lay_kernel,
        in_specs=[vmem, vmem],
        out_specs=vmem,
        out_shape=jax.ShapeDtypeStruct((pieces, ROWS, 2 * n_exp * width + LANES), BF16),
        name="lay_rows",
    )(slots, meta)

    weights = (w_gate.transpose(0, 2, 1), w_up.transpose(0, 2, 1), w_down, proj_in, proj_hidden.T)
    acc_shape = (n_dp, 3 * rank * rank // LANES, LANES)
    half = pieces // 2
    whole = lambda buf: [(buf, 0, pieces)]
    run = lambda blocks, acc: step(blocks, me, weights, acc, acc_shape)
    b10, b30, b01, b03 = shift(own, 0, 1), shift(own, 0, -1), shift(own, 1, 1), shift(own, 1, -1)
    b11, b33, b13, b31 = shift(b10, 1, 1), shift(b30, 1, -1), shift(b03, 0, 1), shift(b01, 0, -1)
    acc = run(
        {(0, 0): whole(own), (1, 0): whole(b10), (3, 0): whole(b30), (0, 1): whole(b01), (0, 3): whole(b03)}, None
    )
    b11, b33, b13, b31, acc = after(acc, b11, b33, b13, b31)
    b21, b23, b12, b32 = shift(b11, 0, 1), shift(b33, 0, -1), shift(b13, 1, -1), shift(b31, 1, 1)
    acc = run({(1, 1): whole(b11), (3, 3): whole(b33), (1, 3): whole(b13), (3, 1): whole(b31)}, acc)
    b21, b23, b12, b32, acc = after(acc, b21, b23, b12, b32)
    cat = lambda *parts: jnp.concatenate(parts, axis=0)
    east, west = shift(cat(b10[:half], b12[0:1]), 0, 1), shift(cat(b30[half:], b32[1:2]), 0, -1)
    north, south = shift(cat(b01[:half], b21[2:3]), 1, 1), shift(cat(b03[half:], b23[3:4]), 1, -1)
    acc = run({(2, 1): whole(b21), (2, 3): whole(b23), (1, 2): whole(b12), (3, 2): whole(b32)}, acc)
    acc = run(
        {
            (2, 0): [(east, 0, half), (west, 0, half)],
            (0, 2): [(north, 0, half), (south, 0, half)],
            (2, 2): [(q, half, 1) for q in (east, west, north, south)],
        },
        acc,
    )

    share = acc.reshape(n_dp, n_dp, -1, LANES).transpose(1, 2, 0, 3)
    share = lax.all_to_all(share.astype(BF16), "dp", split_axis=0, concat_axis=0, tiled=True)
    total = jnp.sum(share.astype(F32), axis=0)
    return total.transpose(1, 0, 2).reshape(n_dp, 1, -1)


def solution(mesh):
    return jax.shard_map(
        per_device,
        mesh=mesh,
        in_specs=(
            P("dp", "expert"),
            P("dp", "expert"),
            P("dp", None),
            P("dp", None),
            P("expert", None, "dp"),
            P("expert", None, "dp"),
            P("expert", "dp", None),
            P(),
            P("dp", None),
        ),
        out_specs=P(None, "expert", "dp"),
        check_vma=False,
    )
```
